256 devices in a mesh: dp: 8 (over z_lo, core), expert: 32 (over y, z_hi, x).
Axes of the slice: x: 4, y: 4, z: 8 (z_hi: 2, z_lo: 4; z = z_hi * 4 + z_lo), core: 2. Of those that a mesh axis runs over, the one named last changes fastest.
Arguments:
- patches_in: bfloat16 [256, 256, 1024], P(('dp', 'expert')), may hold values from -12 to 12
- slot_params: bfloat16 [1024, 256], replicated, may hold values from -2 to 2
- w_in: bfloat16 [64, 1024, 4096], P('expert', None, 'dp'), may hold values from -0.1875 to 0.1875
- w_out: bfloat16 [64, 4096, 1024], P('expert', 'dp'), may hold values from -0.09375 to 0.09375
- grad_out: bfloat16 [256, 256, 1024], P(('dp', 'expert')), may hold values from -6 to 6
Outputs:
- layer_out: bfloat16 [256, 256, 1024], P(('dp', 'expert'))
- grad_x: bfloat16 [256, 256, 1024], P(('dp', 'expert'))
- grad_phi: float32 [1024, 256], replicated
- grad_w_in: bfloat16 [64, 1024, 4096], P('expert', None, 'dp')
- grad_w_out: bfloat16 [64, 4096, 1024], P('expert', 'dp')
The draws below stay inside these ranges and needn't reach their ends.
All inputs are finite; a program needn't handle non-finite values.
Results may differ from the reference program's by a relative error of at most 0.02.
Values may be sent and summed in bfloat16 or wider, within the bound.
No kernel may reach another device: no remote copies, remote signals or barrier semaphores. Data moves between devices by JAX's collectives and lax.ppermute only.
A program may use at most 128 MiB of HBM per device.

```python
import jax
import jax.numpy as jnp
from jax import lax

D = 1024
HID = 4096
PATCHES = 256
SLOTS = 4
EXPERTS = 64
ES = 256
IMAGES = 256
N_DP = 8


def draw_patches_in(key, part):
    key = jax.random.fold_in(key, 11)
    first_key = jax.random.fold_in(key, 0)
    base = jax.random.normal(first_key, (IMAGES, PATCHES, D), jnp.float32)
    base = jnp.clip(base, -6.0, 6.0)
    return jnp.clip(base, -12.0, 12.0).astype(jnp.bfloat16)


def draw_slot_params(key, part):
    key = jax.random.fold_in(key, 12)
    first_key = jax.random.fold_in(key, 0)
    base = jax.random.normal(first_key, (D, ES), jnp.float32) * (1.5 / jnp.sqrt(1.0 * D))
    return jnp.clip(base, -2.0, 2.0).astype(jnp.bfloat16)


def levels(own_key, shape, pieces, smallest, top_value):
    loudness, own = 1.0, jax.random.fold_in(own_key, 6)
    for dim, blocks in pieces:
        steps = jnp.exp(jax.random.uniform(jax.random.fold_in(own, dim), (blocks,), jnp.float32, smallest / len(pieces), top_value / len(pieces)))
        loudness = loudness * jnp.repeat(steps, shape[dim] // blocks).reshape([-1 if axis == dim else 1 for axis in range(len(shape))])
    return loudness


def centred(rng, shape, spread, most, cuts=(), kind=jnp.bfloat16):
    result = jax.random.normal(rng, shape, jnp.float32) * spread
    if len(cuts) > 0:
        result = levels(rng, shape, cuts, -0.22, 0.18) * result
    return jnp.clip(result, min=-most, max=most).astype(kind)


def setup_inputs(seed: int = 0) -> dict:
    keys = jax.random.split(jax.random.key(seed), 6)
    return {
        "patches_in": draw_patches_in(jax.random.fold_in(keys[5], 71), 0),
        "slot_params": draw_slot_params(jax.random.fold_in(keys[5], 71), 0),
        "w_in": centred(keys[2], (EXPERTS, D, HID), D ** -0.5, 0.1875, ((0, 32), (2, 8))),
        "w_out": centred(keys[3], (EXPERTS, HID, D), HID ** -0.5, 0.09375, ((0, 32), (1, 8))),
        "grad_out": centred(keys[4], (IMAGES, PATCHES, D), 1.0, 6.0, ((0, 256),)),
    }


def gelu_tanh(value):
    return jax.nn.gelu(value, approximate=True)

def gelu_slope(value):
    return jax.vjp(gelu_tanh, value)[1](jnp.ones_like(value))[0]

def to_experts(array):
    return array.reshape(IMAGES, EXPERTS, SLOTS, D).transpose(1, 0, 2, 3).reshape(EXPERTS, IMAGES * SLOTS, D)

def to_images(array):
    return array.reshape(EXPERTS, IMAGES, SLOTS, D).transpose(1, 0, 2, 3).reshape(IMAGES, ES, D)

def block_sum(parts):
    parts = lax.optimization_barrier(parts.astype(jnp.bfloat16))
    return lax.optimization_barrier(jnp.sum(parts.astype(jnp.float32), axis=0)).astype(jnp.bfloat16)

def forward_expert(operands):
    rows_in, first, second = operands
    block = HID // N_DP
    preact = jnp.dot(rows_in, first, preferred_element_type=jnp.float32)
    hidden_act = gelu_tanh(preact).astype(jnp.bfloat16)
    parts = jnp.einsum('rkh,khd->krd', hidden_act.reshape(-1, N_DP, block).astype(jnp.float32), second.reshape(N_DP, block, D).astype(jnp.float32))
    return block_sum(parts)

def backward_expert(operands):
    rows_in, first, second, d_rows = operands
    block = HID // N_DP
    preact = jnp.dot(rows_in, first, preferred_element_type=jnp.float32)
    hidden_act = gelu_tanh(preact).astype(jnp.bfloat16)
    d_hidden = (jnp.dot(d_rows, second.T, preferred_element_type=jnp.float32) * gelu_slope(preact)).astype(jnp.bfloat16)
    grad_second = jnp.dot(hidden_act.T, d_rows, preferred_element_type=jnp.float32).astype(jnp.bfloat16)
    grad_first = jnp.dot(rows_in.T, d_hidden, preferred_element_type=jnp.float32).astype(jnp.bfloat16)
    parts = jnp.einsum('rkh,dkh->krd', d_hidden.reshape(-1, N_DP, block).astype(jnp.float32), first.reshape(D, N_DP, block).astype(jnp.float32))
    return (block_sum(parts), grad_first, grad_second)

def reference(patches_in, slot_params, w_in, w_out, grad_out):
    inputs32 = patches_in.astype(jnp.float32)
    phi32 = slot_params.astype(jnp.float32)
    logits = jnp.einsum('bmd,dc->bmc', inputs32, phi32)
    disp_prob = jax.nn.softmax(logits, axis=1)
    comb_prob = jax.nn.softmax(logits, axis=2)
    dispatch = disp_prob.astype(jnp.bfloat16)
    combine = comb_prob.astype(jnp.bfloat16)
    slot_in = jnp.einsum('bmc,bmd->bcd', dispatch.astype(jnp.float32), inputs32).astype(jnp.bfloat16)
    expert_rows = to_experts(slot_in)
    slot_out = to_images(lax.map(forward_expert, (expert_rows, w_in, w_out)))
    layer_out = jnp.einsum('bmc,bcd->bmd', combine.astype(jnp.float32), slot_out.astype(jnp.float32)).astype(jnp.bfloat16)
    grad32 = grad_out.astype(jnp.float32)
    d_comb = jnp.einsum('bmd,bcd->bmc', grad32, slot_out.astype(jnp.float32))
    d_slot_out = jnp.einsum('bmc,bmd->bcd', combine.astype(jnp.float32), grad32).astype(jnp.bfloat16)
    d_logit_comb = (comb_prob * (d_comb - lax.optimization_barrier(jnp.sum(d_comb * comb_prob, axis=2, keepdims=True)))).astype(jnp.bfloat16)
    d_slot_e, grad_w_in, grad_w_out = lax.map(backward_expert, (expert_rows, w_in, w_out, to_experts(d_slot_out)))
    d_slot_in = to_images(d_slot_e).astype(jnp.float32)
    d_disp = jnp.einsum('bmd,bcd->bmc', inputs32, d_slot_in)
    dx_disp = jnp.einsum('bmc,bcd->bmd', dispatch.astype(jnp.float32), d_slot_in)
    d_logit_disp = (disp_prob * (d_disp - lax.optimization_barrier(jnp.sum(d_disp * disp_prob, axis=1, keepdims=True)))).astype(jnp.bfloat16)
    comb32 = d_logit_comb.astype(jnp.float32)
    disp32 = d_logit_disp.astype(jnp.float32)
    grad_x = (dx_disp + jnp.einsum('bmc,dc->bmd', comb32, phi32) + jnp.einsum('bmc,dc->bmd', disp32, phi32)).astype(jnp.bfloat16)
    grad_phi = jnp.einsum('bmd,bmc->dc', inputs32, comb32) + jnp.einsum('bmd,bmc->dc', inputs32, disp32)
    return (layer_out, grad_x, grad_phi, grad_w_in, grad_w_out)
```

```python
import jax
import jax.numpy as jnp
import ml_dtypes
import numpy as np
from jax import lax
from jax.sharding import Mesh
from jax.sharding import PartitionSpec as P

BF16, F32 = jnp.bfloat16, jnp.float32
ZL, ZH, NX, NY, OWNED, SLOTS = 4, 2, 4, 4, 2, 4
NZ, PLANE = ZL * ZH, NX * NY
DP, EXPERT = ("zl", "core"), ("y", "zh", "x")


def z_rank(z):
    z %= NZ
    return (z % ZL) * ZH + z // ZL


def swap_core(value):
    return lax.ppermute(value, "core", [(0, 1), (1, 0)])


def dot(spec, a, b, kind=F32):
    return jnp.einsum(spec, a, b, preferred_element_type=F32).astype(kind)


def one_hot_rows(order):
    return np.eye(len(order), dtype=np.float32)[order].astype(ml_dtypes.bfloat16)


def slot_order():
    index = np.arange(NY * ZH * NX * OWNED * SLOTS).reshape(NY, ZH, NX, OWNED * SLOTS)
    return index.transpose(0, 2, 1, 3).reshape(-1)


def plane_order():
    index = np.arange(PLANE * ZH * OWNED * SLOTS).reshape(PLANE, ZH, OWNED, SLOTS)
    return index.transpose(1, 2, 0, 3).reshape(-1)


def move_z(value, sign):
    pairs = [(z_rank(z), z_rank(z + sign)) for z in range(NZ)]
    return lax.ppermute(value, ("zl", "zh"), pairs)


def ordered(value, after):
    return value if after is None else lax.optimization_barrier((value, after))[0]


def gather_z(rows, mine, after=None):
    rows = ordered(rows, after)
    right, left = {}, {}
    for half in range(ZH):
        right[half, 0] = left[half, 0] = rows[half]
    for step in range(1, NZ // 2):
        for half in range(ZH):
            right[half, step] = move_z(right[half, step - 1], 1)
            left[half, step] = move_z(left[half, step - 1], -1)
    far = NZ // 2
    for half in range(ZH):
        right[half, far] = move_z(right[half, far - 1][:1], 1)
        left[half, far] = move_z(left[half, far - 1][1:], -1)
    halves = []
    for half in range(ZH):
        blocks = [right[half, step] for step in range(far)] + [left[half, step] for step in range(1, far)]
        blocks.append(jnp.concatenate([right[half, far], left[half, far]], axis=0))
        halves.append(jnp.concatenate(blocks, axis=1))
    late = [moved[half, far - 1] for moved in (right, left) for half in range(ZH)]
    return jnp.where(mine[0], halves[0], halves[1]), late


def scatter_z(parts, mine, after=None):
    parts = ordered(parts, after)
    rows = parts.shape[1] // NZ

    def part(half, block):
        value = parts[:, block * rows : (block + 1) * rows]
        return jnp.where(mine[half], value, jnp.zeros_like(value))

    far = NZ // 2
    down, up = {}, {}
    for half in range(ZH):
        whole = part(half, NZ - 1)
        down[half] = move_z(whole[:1], -1)
        up[half] = move_z(whole[1:], 1)
    for step in range(far - 1, 0, -1):
        for half in range(ZH):
            to_below, to_above = part(half, step), part(half, far - 1 + step)
            if step == far - 1:
                to_below = jnp.concatenate([to_below[:1] + down[half], to_below[1:]], axis=0)
                to_above = jnp.concatenate([to_above[:1], to_above[1:] + up[half]], axis=0)
            else:
                to_below, to_above = to_below + down[half], to_above + up[half]
            down[half] = move_z(to_below, -1)
            up[half] = move_z(to_above, 1)
        if step == 2:
            late = [*down.values(), *up.values()]
    sums = []
    for half in range(ZH):
        total = part(half, 0).astype(F32) + down[half].astype(F32) + up[half].astype(F32)
        sums.append(total.astype(BF16))
    return jnp.stack(sums), late


def swap_plane(value):
    return lax.all_to_all(value, ("y", "x"), 0, 0, tiled=True)


def to_experts(slots, order):
    width = slots.shape[-1]
    arrived = swap_plane(slots.reshape(PLANE, -1, width)).reshape(-1, width)
    return dot("rk,kd->rd", order, arrived, BF16).reshape(ZH, OWNED, -1, width)


def to_images(rows, order):
    width = rows.shape[-1]
    placed = dot("kr,kd->rd", order, rows.reshape(-1, width), BF16)
    return swap_plane(placed.reshape(PLANE, -1, width)).reshape(-1, width)


def total_over_devices(value, core):
    half = value.shape[0] // 2
    keep = lax.dynamic_slice_in_dim(value, core * half, half)
    give = lax.dynamic_slice_in_dim(value, (1 - core) * half, half)
    chip = keep + swap_core(give.astype(BF16)).astype(F32)
    blocks = swap_plane(chip.astype(BF16).reshape(PLANE, half // PLANE, -1))
    block = jnp.sum(blocks.astype(F32), axis=0)
    for flip in (1, 2):
        block = block + lax.ppermute(block, "zl", [(z, z ^ flip) for z in range(ZL)])
    block = block + lax.ppermute(block, "zh", [(0, 1), (1, 0)])
    block = block.astype(BF16)
    own = swap_plane(jnp.broadcast_to(block[None], (PLANE, *block.shape))).reshape(half, -1)
    other = swap_core(own)
    own, other = own.astype(F32), other.astype(F32)
    return jnp.where(core == 0, jnp.concatenate([own, other]), jnp.concatenate([other, own]))


def gelu(value):
    return jax.nn.gelu(value, approximate=True)


def gelu_slope(value):
    return jax.vjp(gelu, value)[1](jnp.ones_like(value))[0]


def on_device(patches_in, slot_params, w_in, w_out, grad_out):
    core, zh = lax.axis_index("core"), lax.axis_index("zh")
    mine = [zh == half for half in range(ZH)]
    tokens, grad = patches_in[0], grad_out[0]
    slot_rows = jnp.asarray(one_hot_rows(slot_order()))
    plane_rows = jnp.asarray(one_hot_rows(plane_order()))

    phi = dot("dc,kc->dk", slot_params, slot_rows, BF16)
    logits = dot("md,dc->mc", tokens, phi)
    disp_prob = jax.nn.softmax(logits, axis=0)
    comb_prob = jax.nn.softmax(logits, axis=1)
    dispatch, combine = disp_prob.astype(BF16), comb_prob.astype(BF16)
    slot_in = dot("mc,md->cd", dispatch, tokens, BF16)
    d_slot_out = dot("mc,md->cd", combine, grad, BF16)

    first = jnp.concatenate([w_in, swap_core(w_in)], axis=2)
    second = jnp.concatenate([w_out, swap_core(w_out)], axis=1)
    hidden = w_in.shape[2]

    rows, late = gather_z(to_experts(slot_in, plane_rows), mine)
    d_rows, late = gather_z(to_experts(d_slot_out, plane_rows), mine, late)

    preact = dot("erd,edh->erh", rows, first)
    hidden_act = gelu(preact).astype(BF16)
    out_part = dot("erh,ehd->erd", hidden_act, second, BF16)
    slot_sums, late = scatter_z(out_part, mine, late)
    slot_out = to_images(slot_sums, plane_rows)

    d_hidden = (dot("erd,ehd->erh", d_rows, second) * gelu_slope(preact)).astype(BF16)
    in_part = dot("erh,edh->erd", d_hidden, first, BF16)
    slot_sums, late = scatter_z(in_part, mine, late)
    d_slot_in = to_images(slot_sums, plane_rows)

    grad_first = dot("erd,erh->edh", rows, d_hidden)
    grad_first = grad_first[:, :, :hidden] + swap_core(grad_first[:, :, hidden:].astype(BF16)).astype(F32)
    grad_second = dot("erh,erd->ehd", hidden_act, d_rows)
    grad_second = grad_second[:, :hidden] + swap_core(grad_second[:, hidden:].astype(BF16)).astype(F32)

    layer_out = dot("mc,cd->md", combine, slot_out, BF16)
    d_comb = dot("md,cd->mc", grad, slot_out)
    d_logit_comb = (comb_prob * (d_comb - jnp.sum(d_comb * comb_prob, axis=1, keepdims=True))).astype(BF16)
    grad_x = dot("mc,dc->md", d_logit_comb, phi)
    grad_phi = dot("md,mc->dc", tokens, dot("mk,kc->mc", d_logit_comb, slot_rows, BF16))

    d_disp = dot("md,cd->mc", tokens, d_slot_in)
    d_logit_disp = (disp_prob * (d_disp - jnp.sum(d_disp * disp_prob, axis=0, keepdims=True))).astype(BF16)
    grad_x = grad_x + dot("mc,cd->md", dispatch, d_slot_in) + dot("mc,dc->md", d_logit_disp, phi)
    grad_phi = grad_phi + dot("md,mc->dc", tokens, dot("mk,kc->mc", d_logit_disp, slot_rows, BF16))
    grad_phi = total_over_devices(grad_phi, core)
    return layer_out[None], grad_x.astype(BF16)[None], grad_phi, grad_first.astype(BF16), grad_second.astype(BF16)


def solution(mesh):
    fine = Mesh(mesh.devices.reshape(ZL, 2, NY, ZH, NX), ("zl", "core", "y", "zh", "x"))
    images = P((*DP, *EXPERT), None, None)
    placed = (images, P(), P(EXPERT, None, DP), P(EXPERT, DP, None), images)
    return jax.shard_map(
        on_device,
        mesh=fine,
        in_specs=placed,
        out_specs=(images, images, P(), placed[2], placed[3]),
        check_vma=False,
    )
```

```python
import jax
import jax.numpy as jnp
import ml_dtypes
import numpy as np
from jax import lax
from jax.sharding import Mesh
from jax.sharding import PartitionSpec as P

BF16, F32 = jnp.bfloat16, jnp.float32
ZL, ZH, NX, NY, OWNED, SLOTS = 4, 2, 4, 4, 2, 4
NZ, PLANE = ZL * ZH, NX * NY
KINDS = 2
DP, EXPERT = ("zl", "core"), ("y", "zh", "x")


def z_rank(z):
    z %= NZ
    return (z % ZL) * ZH + z // ZL


def swap_core(value):
    return lax.ppermute(value, "core", [(0, 1), (1, 0)])


def dot(spec, a, b, kind=F32):
    return jnp.einsum(spec, a, b, preferred_element_type=F32).astype(kind)


def one_hot_rows(order):
    return np.eye(len(order), dtype=np.float32)[order].astype(ml_dtypes.bfloat16)


def slot_order():
    index = np.arange(NY * ZH * NX * OWNED * SLOTS).reshape(NY, ZH, NX, OWNED * SLOTS)
    return index.transpose(0, 2, 1, 3).reshape(-1)


def plane_order():
    index = np.arange(PLANE * KINDS * ZH * OWNED * SLOTS).reshape(PLANE, KINDS, ZH, OWNED, SLOTS)
    return index.transpose(2, 1, 3, 0, 4).reshape(-1)


def move_z(value, sign, planes=range(NZ)):
    pairs = [(z_rank(z), z_rank(z + sign)) for z in planes]
    return lax.ppermute(value, ("zl", "zh"), pairs)


def ordered(value, *after):
    return lax.optimization_barrier((value, after))[0] if after else value


STEPS = 5


def paired(come, step):
    come[1, step], come[-1, step] = lax.optimization_barrier((come[1, step], come[-1, step]))


def gather_z(own, other, up, down, place, early):
    last = {1: place == ZL - 1, -1: place == 0}
    first = {1: up, -1: down}
    come = {}

    def by_kind(blocks):
        return [jnp.concatenate([block[at : at + OWNED] for block in blocks], axis=1) for at in (0, OWNED)]

    for step in range(1, STEPS + 1):
        if step > 1:
            paired(come, step - 1)
        if step == STEPS:
            near = by_kind([own, come[1, 1], come[1, 2], come[-1, 1], come[-1, 2]])
            come[1, step - 1] = ordered(come[1, step - 1], *early(*near))
        for sign in (1, -1):
            value = first[sign] if step == 1 else come[sign, step - 1]
            if step == 2:
                value = jnp.where(last[sign], come[sign, 0], value)
            come[sign, step] = move_z(value, sign)
            if step == 1:
                come[sign, 0] = move_z(other, sign, (2, 6) if sign == 1 else (1, 5))
    far = [jnp.where(place >= step - 2, come[1, step], come[-1, 8 - step]) for step in (3, 4, 5)]
    return near, by_kind(far)


def scatter_z(near, far, place, work):
    rows = far[0].shape[1] // 3
    first = {1: place == 0, -1: place == ZL - 1}
    order = {1: (5, 6, 7, 4, 3), -1: (7, 6, 5, 2, 1)}
    come = {}

    def part(block):
        kinds, at = (near, block) if block < 5 else (far, block - 5)
        return jnp.concatenate([kind[:, at * rows : (at + 1) * rows] for kind in kinds])

    def added(sign, step):
        return jnp.where(first[sign], jnp.zeros_like(come[sign, step]), come[sign, step])

    for step in range(1, STEPS + 1):
        if step > 1:
            paired(come, step - 1)
            come[1, step - 1] = ordered(come[1, step - 1], *work(step, come[1, step - 1]))
        for sign in (1, -1):
            value = part(order[sign][step - 1])
            if step > 1:
                value = value + added(sign, step - 1)
            come[sign, step] = move_z(value, sign)
            if step == STEPS:
                come[sign, 0] = move_z(come[sign, STEPS - 1], sign, (0, 4) if sign == 1 else (3, 7))
    come[-1, STEPS] = ordered(come[-1, STEPS], *work(STEPS + 1, come[1, STEPS]))
    own = part(0).astype(F32) + added(1, STEPS).astype(F32) + added(-1, STEPS).astype(F32)
    from_below = jnp.where(place == 0, come[1, STEPS], come[1, 0])
    from_above = jnp.where(place == 2, come[-1, 0], come[-1, STEPS])
    return own.astype(BF16), jnp.where(place < 2, from_below, from_above)


def swap_plane(value):
    return lax.all_to_all(value, ("y", "x"), 0, 0, tiled=True)


def to_experts(slots, order, half, place):
    width = slots.shape[-1]
    sent = slots.reshape(KINDS, PLANE, -1, width).transpose(1, 0, 2, 3).reshape(PLANE, -1, width)
    arrived = swap_plane(sent).reshape(-1, width)
    low, high = jnp.split(order, 2)
    own, other = jnp.where(half == 0, low, high), jnp.where(half == 0, high, low)
    up, down = jnp.where(place == ZL - 1, other, own), jnp.where(place == 0, other, own)
    rows = jnp.concatenate([own, other, up, down])
    return dot("rk,kd->rd", rows, arrived, BF16).reshape(4, KINDS * OWNED, -1, width)


def to_images(own, other, order, half):
    width = own.shape[-1]
    low, high = jnp.where(half == 0, own, other), jnp.where(half == 0, other, own)
    rows = jnp.concatenate([low, high]).reshape(-1, width)
    arrived = swap_plane(dot("kr,kd->rd", order, rows, BF16).reshape(PLANE, -1, width))
    return [kind.reshape(-1, width) for kind in jnp.split(arrived, KINDS, axis=1)]


def total_over_devices(value, core):
    half = value.shape[0] // 2
    keep = lax.dynamic_slice_in_dim(value, core * half, half)
    give = lax.dynamic_slice_in_dim(value, (1 - core) * half, half)
    chip = keep + swap_core(give.astype(BF16)).astype(F32)
    blocks = swap_plane(chip.astype(BF16).reshape(PLANE, half // PLANE, -1))
    block = jnp.sum(blocks.astype(F32), axis=0)
    for flip in (1, 2):
        block = block + lax.ppermute(block, "zl", [(z, z ^ flip) for z in range(ZL)])
    block = block + lax.ppermute(block, "zh", [(0, 1), (1, 0)])
    block = block.astype(BF16)
    own = swap_plane(jnp.broadcast_to(block[None], (PLANE, *block.shape))).reshape(half, -1)
    other = swap_core(own)
    own, other = own.astype(F32), other.astype(F32)
    return jnp.where(core == 0, jnp.concatenate([own, other]), jnp.concatenate([other, own]))


def gelu(value):
    return jax.nn.gelu(value, approximate=True)


def gelu_slope(value):
    return jax.vjp(gelu, value)[1](jnp.ones_like(value))[0]


def on_device(patches_in, slot_params, w_in, w_out, grad_out):
    core, half, place = lax.axis_index("core"), lax.axis_index("zh"), lax.axis_index("zl")
    tokens, grad = patches_in[0], grad_out[0]
    slot_rows = jnp.asarray(one_hot_rows(slot_order()))
    plane_rows = jnp.asarray(one_hot_rows(plane_order()))

    phi = dot("dc,kc->dk", slot_params, slot_rows, BF16)
    logits = dot("md,dc->mc", tokens, phi)
    disp_prob = jax.nn.softmax(logits, axis=0)
    comb_prob = jax.nn.softmax(logits, axis=1)
    dispatch, combine = disp_prob.astype(BF16), comb_prob.astype(BF16)
    slot_in = dot("mc,md->cd", dispatch, tokens, BF16)
    d_slot_out = dot("mc,md->cd", combine, grad, BF16)

    first = jnp.concatenate([w_in, swap_core(w_in)], axis=2)
    second = jnp.concatenate([w_out, swap_core(w_out)], axis=1)
    hidden = w_in.shape[2]

    sent = to_experts(jnp.stack([slot_in, d_slot_out]), plane_rows, half, place)

    def through(rows, d_rows):
        preact = dot("erd,edh->erh", rows, first)
        hidden_act = gelu(preact).astype(BF16)
        out_part = dot("erh,ehd->erd", hidden_act, second, BF16)
        d_hidden = (dot("erd,ehd->erh", d_rows, second) * gelu_slope(preact)).astype(BF16)
        in_part = dot("erh,edh->erd", d_hidden, first, BF16)
        return hidden_act, d_hidden, out_part, in_part

    made = []

    def early(rows, d_rows):
        made.append(through(rows, d_rows))
        return made[0]

    near, far = gather_z(*sent, place, early)
    made.append(through(*far))
    rows, d_rows = (jnp.concatenate(pair, axis=1) for pair in zip(near, far))
    hidden_act, d_hidden = (jnp.concatenate(pair, axis=1) for pair in list(zip(*made))[:2])
    in_part = made[1][3]

    done = {}

    def work(step, arrived):
        if step == 2:
            done["second"] = dot("erh,erd->ehd", ordered(hidden_act, in_part), d_rows, BF16)
            return [done["second"]]
        if step == 3:
            done["first"] = dot("erd,erh->edh", rows, ordered(d_hidden, done["second"]), BF16)
            return [done["first"]]
        if step == 4:
            return []
        if step == 5:
            give = swap_core(done["second"][:, hidden:])
            done["second"] = (done["second"][:, :hidden].astype(F32) + give.astype(F32)).astype(BF16)
            return [done["second"]]
        give = swap_core(done["first"][:, :, hidden:])
        done["first"] = (done["first"][:, :, :hidden].astype(F32) + give.astype(F32)).astype(BF16)
        return [done["first"]]

    slot_out, d_slot_in = to_images(*scatter_z(made[0][2:], made[1][2:], place, work), plane_rows, half)
    grad_first, grad_second = done["first"], done["second"]

    layer_out = dot("mc,cd->md", combine, slot_out, BF16)
    d_comb = dot("md,cd->mc", grad, slot_out)
    d_logit_comb = (comb_prob * (d_comb - jnp.sum(d_comb * comb_prob, axis=1, keepdims=True))).astype(BF16)
    grad_x = dot("mc,dc->md", d_logit_comb, phi)
    grad_phi = dot("md,mc->dc", tokens, dot("mk,kc->mc", d_logit_comb, slot_rows, BF16))

    d_disp = dot("md,cd->mc", tokens, d_slot_in)
    d_logit_disp = (disp_prob * (d_disp - jnp.sum(d_disp * disp_prob, axis=0, keepdims=True))).astype(BF16)
    grad_x = grad_x + dot("mc,cd->md", dispatch, d_slot_in) + dot("mc,dc->md", d_logit_disp, phi)
    grad_phi = grad_phi + dot("md,mc->dc", tokens, dot("mk,kc->mc", d_logit_disp, slot_rows, BF16))
    grad_phi = total_over_devices(grad_phi, core)
    return layer_out[None], grad_x.astype(BF16)[None], grad_phi, grad_first, grad_second


def solution(mesh):
    fine = Mesh(mesh.devices.reshape(ZL, 2, NY, ZH, NX), ("zl", "core", "y", "zh", "x"))
    images = P((*DP, *EXPERT), None, None)
    placed = (images, P(), P(EXPERT, None, DP), P(EXPERT, DP, None), images)
    return jax.shard_map(
        on_device,
        mesh=fine,
        in_specs=placed,
        out_specs=(images, images, P(), placed[2], placed[3]),
        check_vma=False,
    )
```

```python
import jax
import jax.numpy as jnp
import ml_dtypes
import numpy as np
from jax import lax
from jax.sharding import Mesh
from jax.sharding import PartitionSpec as P

BF16, F32 = jnp.bfloat16, jnp.float32
ZL, ZH, NX, NY, OWNED, SLOTS = 4, 2, 4, 4, 2, 4
NZ, PLANE = ZL * ZH, NX * NY
KINDS = 2
DP, EXPERT = ("zl", "core"), ("y", "zh", "x")


def z_rank(z):
    z %= NZ
    return (z % ZL) * ZH + z // ZL


def swap_core(value):
    return lax.ppermute(value, "core", [(0, 1), (1, 0)])


def dot(spec, a, b, kind=F32):
    return jnp.einsum(spec, a, b, preferred_element_type=F32).astype(kind)


def one_hot_rows(order):
    return np.eye(len(order), dtype=np.float32)[order].astype(ml_dtypes.bfloat16)


def slot_order():
    index = np.arange(NY * ZH * NX * OWNED * SLOTS).reshape(NY, ZH, NX, OWNED * SLOTS)
    return index.transpose(0, 2, 1, 3).reshape(-1)


def plane_order():
    index = np.arange(PLANE * KINDS * ZH * OWNED * SLOTS).reshape(PLANE, KINDS, ZH, OWNED, SLOTS)
    return index.transpose(2, 1, 3, 0, 4).reshape(-1)


def move_z(value, sign, planes=range(NZ)):
    pairs = [(z_rank(z), z_rank(z + sign)) for z in planes]
    return lax.ppermute(value, ("zl", "zh"), pairs)


def ordered(value, *after):
    return lax.optimization_barrier((value, after))[0] if after else value


STEPS = 5


def paired(come, step):
    come[1, step], come[-1, step] = lax.optimization_barrier((come[1, step], come[-1, step]))


def gather_z(own, other, up, down, place, early):
    last = {1: place == ZL - 1, -1: place == 0}
    first = {1: up, -1: down}
    come = {}

    def by_kind(blocks):
        return [jnp.concatenate([block[at : at + OWNED] for block in blocks], axis=1) for at in (0, OWNED)]

    for step in range(1, STEPS + 1):
        if step > 1:
            paired(come, step - 1)
        if step == STEPS:
            near = by_kind([own, come[1, 1], come[1, 2], come[-1, 1], come[-1, 2]])
            come[1, step - 1] = ordered(come[1, step - 1], *early(*near))
        for sign in (1, -1):
            value = first[sign] if step == 1 else come[sign, step - 1]
            if step == 2:
                value = jnp.where(last[sign], come[sign, 0], value)
            come[sign, step] = move_z(value, sign)
            if step == 1:
                come[sign, 0] = move_z(other, sign, (2, 6) if sign == 1 else (1, 5))
    far = [jnp.where(place >= step - 2, come[1, step], come[-1, 8 - step]) for step in (3, 4, 5)]
    return near, by_kind(far)


def scatter_z(near, far, place, work):
    rows = far[0].shape[1] // 3
    first = {1: place == 0, -1: place == ZL - 1}
    order = {1: (5, 6, 7, 4, 3), -1: (7, 6, 5, 2, 1)}
    come = {}

    def part(block):
        kinds, at = (near, block) if block < 5 else (far, block - 5)
        return jnp.concatenate([kind[:, at * rows : (at + 1) * rows] for kind in kinds])

    def added(sign, step):
        return jnp.where(first[sign], jnp.zeros_like(come[sign, step]), come[sign, step])

    for step in range(1, STEPS + 1):
        if step > 1:
            paired(come, step - 1)
            come[1, step - 1] = ordered(come[1, step - 1], *work(step, come[1, step - 1]))
        if step == STEPS - 1:
            come[1, step - 1] = ordered(come[1, step - 1], *beside)
        for sign in (1, -1):
            value = part(order[sign][step - 1])
            if step == STEPS:
                arrived = come[sign, step - 1]
                value = jnp.where(first[sign], arrived, value + arrived)
            elif step > 1:
                value = value + added(sign, step - 1)
            come[sign, step] = move_z(value, sign)
        if step == 1:
            beside = move_z(part(order[1][-1]), 1, (0, 4)), move_z(part(order[-1][-1]), -1, (3, 7))
    come[-1, STEPS] = ordered(come[-1, STEPS], *work(STEPS + 1, come[1, STEPS]))
    nothing = jnp.zeros_like(beside[0])
    below = jnp.where(place == 0, nothing, jnp.where(place == 1, beside[0], come[1, STEPS]))
    above = jnp.where(place == ZL - 1, nothing, jnp.where(place == 2, beside[1], come[-1, STEPS]))
    own = part(0).astype(F32) + below.astype(F32) + above.astype(F32)
    return own.astype(BF16), jnp.where(place < 2, come[1, STEPS], come[-1, STEPS])


def swap_plane(value):
    return lax.all_to_all(value, ("y", "x"), 0, 0, tiled=True)


def to_experts(slots, order, half, place):
    width = slots.shape[-1]
    sent = slots.reshape(KINDS, PLANE, -1, width).transpose(1, 0, 2, 3).reshape(PLANE, -1, width)
    arrived = swap_plane(sent).reshape(-1, width)
    low, high = jnp.split(order, 2)
    own, other = jnp.where(half == 0, low, high), jnp.where(half == 0, high, low)
    up, down = jnp.where(place == ZL - 1, other, own), jnp.where(place == 0, other, own)
    rows = jnp.concatenate([own, other, up, down])
    return dot("rk,kd->rd", rows, arrived, BF16).reshape(4, KINDS * OWNED, -1, width)


def to_images(own, other, order, half):
    width = own.shape[-1]
    low, high = jnp.where(half == 0, own, other), jnp.where(half == 0, other, own)
    rows = jnp.concatenate([low, high]).reshape(-1, width)
    arrived = swap_plane(dot("kr,kd->rd", order, rows, BF16).reshape(PLANE, -1, width))
    return [kind.reshape(-1, width) for kind in jnp.split(arrived, KINDS, axis=1)]


def total_over_devices(value, core):
    half = value.shape[0] // 2
    keep = lax.dynamic_slice_in_dim(value, core * half, half)
    give = lax.dynamic_slice_in_dim(value, (1 - core) * half, half)
    chip = keep + swap_core(give.astype(BF16)).astype(F32)
    blocks = swap_plane(chip.astype(BF16).reshape(PLANE, half // PLANE, -1))
    block = jnp.sum(blocks.astype(F32), axis=0)
    for flip in (1, 2):
        block = block + lax.ppermute(block, "zl", [(z, z ^ flip) for z in range(ZL)])
    block = block + lax.ppermute(block, "zh", [(0, 1), (1, 0)])
    block = block.astype(BF16)
    own = swap_plane(jnp.broadcast_to(block[None], (PLANE, *block.shape))).reshape(half, -1)
    other = swap_core(own)
    own, other = own.astype(F32), other.astype(F32)
    return jnp.where(core == 0, jnp.concatenate([own, other]), jnp.concatenate([other, own]))


def gelu(value):
    return jax.nn.gelu(value, approximate=True)


def gelu_slope(value):
    return jax.vjp(gelu, value)[1](jnp.ones_like(value))[0]


def on_device(patches_in, slot_params, w_in, w_out, grad_out):
    core, half, place = lax.axis_index("core"), lax.axis_index("zh"), lax.axis_index("zl")
    tokens, grad = patches_in[0], grad_out[0]
    slot_rows = jnp.asarray(one_hot_rows(slot_order()))
    plane_rows = jnp.asarray(one_hot_rows(plane_order()))

    phi = dot("dc,kc->dk", slot_params, slot_rows, BF16)
    logits = dot("md,dc->mc", tokens, phi)
    disp_prob = jax.nn.softmax(logits, axis=0)
    comb_prob = jax.nn.softmax(logits, axis=1)
    dispatch, combine = disp_prob.astype(BF16), comb_prob.astype(BF16)
    slot_in = dot("mc,md->cd", dispatch, tokens, BF16)
    d_slot_out = dot("mc,md->cd", combine, grad, BF16)

    first = jnp.concatenate([w_in, swap_core(w_in)], axis=2)
    second = jnp.concatenate([w_out, swap_core(w_out)], axis=1)
    hidden = w_in.shape[2]

    sent = to_experts(jnp.stack([slot_in, d_slot_out]), plane_rows, half, place)

    def through(rows, d_rows):
        preact = dot("erd,edh->erh", rows, first)
        hidden_act = gelu(preact).astype(BF16)
        out_part = dot("erh,ehd->erd", hidden_act, second, BF16)
        d_hidden = (dot("erd,ehd->erh", d_rows, second) * gelu_slope(preact)).astype(BF16)
        in_part = dot("erh,edh->erd", d_hidden, first, BF16)
        return hidden_act, d_hidden, out_part, in_part

    made = []

    def early(rows, d_rows):
        made.append(through(rows, d_rows))
        return made[0]

    near, far = gather_z(*sent, place, early)
    made.append(through(*far))
    rows, d_rows = (jnp.concatenate(pair, axis=1) for pair in zip(near, far))
    hidden_act, d_hidden = (jnp.concatenate(pair, axis=1) for pair in list(zip(*made))[:2])
    in_part = made[1][3]

    done = {}

    def work(step, arrived):
        if step == 2:
            done["second"] = dot("erh,erd->ehd", ordered(hidden_act, in_part), d_rows, BF16)
            return [done["second"]]
        if step == 3:
            done["first"] = dot("erd,erh->edh", rows, ordered(d_hidden, done["second"]), BF16)
            return [done["first"]]
        if step <= STEPS:
            return []
        give_second, give_first = swap_core(done["second"][:, hidden:]), swap_core(done["first"][:, :, hidden:])
        done["second"] = (done["second"][:, :hidden].astype(F32) + give_second.astype(F32)).astype(BF16)
        done["first"] = (done["first"][:, :, :hidden].astype(F32) + give_first.astype(F32)).astype(BF16)
        return [done["first"], done["second"]]

    slot_out, d_slot_in = to_images(*scatter_z(made[0][2:], made[1][2:], place, work), plane_rows, half)
    grad_first, grad_second = done["first"], done["second"]

    layer_out = dot("mc,cd->md", combine, slot_out, BF16)
    d_comb = dot("md,cd->mc", grad, slot_out)
    d_logit_comb = (comb_prob * (d_comb - jnp.sum(d_comb * comb_prob, axis=1, keepdims=True))).astype(BF16)
    grad_x = dot("mc,dc->md", d_logit_comb, phi)
    grad_phi = dot("md,mc->dc", tokens, dot("mk,kc->mc", d_logit_comb, slot_rows, BF16))

    d_disp = dot("md,cd->mc", tokens, d_slot_in)
    d_logit_disp = (disp_prob * (d_disp - jnp.sum(d_disp * disp_prob, axis=0, keepdims=True))).astype(BF16)
    grad_x = grad_x + dot("mc,cd->md", dispatch, d_slot_in) + dot("mc,dc->md", d_logit_disp, phi)
    grad_phi = grad_phi + dot("md,mc->dc", tokens, dot("mk,kc->mc", d_logit_disp, slot_rows, BF16))
    grad_phi = total_over_devices(grad_phi, core)
    return layer_out[None], grad_x.astype(BF16)[None], grad_phi, grad_first, grad_second


def solution(mesh):
    fine = Mesh(mesh.devices.reshape(ZL, 2, NY, ZH, NX), ("zl", "core", "y", "zh", "x"))
    images = P((*DP, *EXPERT), None, None)
    placed = (images, P(), P(EXPERT, None, DP), P(EXPERT, DP, None), images)
    return jax.shard_map(
        on_device,
        mesh=fine,
        in_specs=placed,
        out_specs=(images, images, P(), placed[2], placed[3]),
        check_vma=False,
    )
```

```python
import jax
import jax.numpy as jnp
import ml_dtypes
import numpy as np
from jax import lax
from jax.sharding import Mesh
from jax.sharding import PartitionSpec as P

BF16, F32 = jnp.bfloat16, jnp.float32
ZL, ZH, NX, NY, OWNED, SLOTS = 4, 2, 4, 4, 2, 4
NZ, PLANE = ZL * ZH, NX * NY
KINDS = 2
DP, EXPERT = ("zl", "core"), ("y", "zh", "x")


def z_rank(z):
    z %= NZ
    return (z % ZL) * ZH + z // ZL


def swap_core(value):
    return lax.ppermute(value, "core", [(0, 1), (1, 0)])


def dot(spec, a, b, kind=F32):
    return jnp.einsum(spec, a, b, preferred_element_type=F32).astype(kind)


def one_hot_rows(order):
    return np.eye(len(order), dtype=np.float32)[order].astype(ml_dtypes.bfloat16)


def slot_order():
    index = np.arange(NY * ZH * NX * OWNED * SLOTS).reshape(NY, ZH, NX, OWNED * SLOTS)
    return index.transpose(0, 2, 1, 3).reshape(-1)


def plane_order():
    index = np.arange(PLANE * KINDS * ZH * OWNED * SLOTS).reshape(PLANE, KINDS, ZH, OWNED, SLOTS)
    return index.transpose(2, 1, 3, 0, 4).reshape(-1)


def move_z(value, sign, planes=range(NZ)):
    pairs = [(z_rank(z), z_rank(z + sign)) for z in planes]
    return lax.ppermute(value, ("zl", "zh"), pairs)


def ordered(value, *after):
    return lax.optimization_barrier((value, after))[0] if after else value


STEPS = 5


def paired(come, step):
    come[1, step], come[-1, step] = lax.optimization_barrier((come[1, step], come[-1, step]))


def gather_z(own, other, up, down, place, early):
    last = {1: place == ZL - 1, -1: place == 0}
    first = {1: up, -1: down}
    come = {}

    def by_kind(blocks):
        return [jnp.concatenate([block[at : at + OWNED] for block in blocks], axis=1) for at in (0, OWNED)]

    for step in range(1, STEPS + 1):
        if step > 1:
            paired(come, step - 1)
        if step == STEPS:
            near = by_kind([own, come[1, 1], come[1, 2], come[-1, 1], come[-1, 2]])
            come[1, step - 1] = ordered(come[1, step - 1], *early(*near))
        for sign in (1, -1):
            value = first[sign] if step == 1 else come[sign, step - 1]
            if step == 2:
                value = jnp.where(last[sign], come[sign, 0], value)
            hops = range(NZ) if step < STEPS else (2, 6) if sign == 1 else (1, 5)
            come[sign, step] = move_z(value, sign, hops)
            if step == 1:
                come[sign, 0] = move_z(other, sign, (2, 6) if sign == 1 else (1, 5))
    far = [jnp.where(place >= step - 2, come[1, step], come[-1, 8 - step]) for step in (3, 4, 5)]
    return near, by_kind(far)


def send_beside(near):
    rows = near[0].shape[1] // 5
    above, below = (jnp.concatenate([kind[:, at * rows : (at + 1) * rows] for kind in near]) for at in (3, 1))
    return move_z(above, 1, (0, 4)), move_z(below, -1, (3, 7))


def scatter_z(near, far, beside, place, work):
    rows = far[0].shape[1] // 3
    first = {1: place == 0, -1: place == ZL - 1}
    order = {1: (5, 6, 7, 4, 3), -1: (7, 6, 5, 2, 1)}
    come = {}

    def part(block):
        kinds, at = (near, block) if block < 5 else (far, block - 5)
        return jnp.concatenate([kind[:, at * rows : (at + 1) * rows] for kind in kinds])

    def added(sign, step):
        return jnp.where(first[sign], jnp.zeros_like(come[sign, step]), come[sign, step])

    for step in range(1, STEPS + 1):
        if step > 1:
            paired(come, step - 1)
            come[1, step - 1] = ordered(come[1, step - 1], *work(step, come[1, step - 1]))
        if step == 2:
            come[1, step - 1] = ordered(come[1, step - 1], *beside)
        for sign in (1, -1):
            value = part(order[sign][step - 1])
            if step == STEPS:
                arrived = come[sign, step - 1]
                value = jnp.where(first[sign], arrived, value + arrived)
            elif step > 1:
                value = value + added(sign, step - 1)
            come[sign, step] = move_z(value, sign)
    come[-1, STEPS] = ordered(come[-1, STEPS], *work(STEPS + 1, come[1, STEPS]))
    nothing = jnp.zeros_like(beside[0])
    below = jnp.where(place == 0, nothing, jnp.where(place == 1, beside[0], come[1, STEPS]))
    above = jnp.where(place == ZL - 1, nothing, jnp.where(place == 2, beside[1], come[-1, STEPS]))
    own = part(0).astype(F32) + below.astype(F32) + above.astype(F32)
    return own.astype(BF16), jnp.where(place < 2, come[1, STEPS], come[-1, STEPS])


def swap_plane(value):
    return lax.all_to_all(value, ("y", "x"), 0, 0, tiled=True)


def to_experts(slots, order, half, place):
    width = slots.shape[-1]
    sent = slots.reshape(KINDS, PLANE, -1, width).transpose(1, 0, 2, 3).reshape(PLANE, -1, width)
    arrived = swap_plane(sent).reshape(-1, width)
    low, high = jnp.split(order, 2)
    own, other = jnp.where(half == 0, low, high), jnp.where(half == 0, high, low)
    up, down = jnp.where(place == ZL - 1, other, own), jnp.where(place == 0, other, own)
    rows = jnp.concatenate([own, other, up, down])
    return dot("rk,kd->rd", rows, arrived, BF16).reshape(4, KINDS * OWNED, -1, width)


def to_images(own, other, order, half):
    width = own.shape[-1]
    low, high = jnp.where(half == 0, own, other), jnp.where(half == 0, other, own)
    rows = jnp.concatenate([low, high]).reshape(-1, width)
    arrived = swap_plane(dot("kr,kd->rd", order, rows, BF16).reshape(PLANE, -1, width))
    return [kind.reshape(-1, width) for kind in jnp.split(arrived, KINDS, axis=1)]


def total_over_devices(value, core):
    half = value.shape[0] // 2
    keep = lax.dynamic_slice_in_dim(value, core * half, half)
    give = lax.dynamic_slice_in_dim(value, (1 - core) * half, half)
    chip = keep + swap_core(give.astype(BF16)).astype(F32)
    blocks = swap_plane(chip.astype(BF16).reshape(PLANE, half // PLANE, -1))
    block = jnp.sum(blocks.astype(F32), axis=0)
    for flip in (1, 2):
        block = block + lax.ppermute(block, "zl", [(z, z ^ flip) for z in range(ZL)])
    block = block + lax.ppermute(block, "zh", [(0, 1), (1, 0)])
    block = block.astype(BF16)
    own = swap_plane(jnp.broadcast_to(block[None], (PLANE, *block.shape))).reshape(half, -1)
    other = swap_core(own)
    own, other = own.astype(F32), other.astype(F32)
    return jnp.where(core == 0, jnp.concatenate([own, other]), jnp.concatenate([other, own]))


def gelu(value):
    return jax.nn.gelu(value, approximate=True)


def gelu_slope(value):
    return jax.vjp(gelu, value)[1](jnp.ones_like(value))[0]


def on_device(patches_in, slot_params, w_in, w_out, grad_out):
    core, half, place = lax.axis_index("core"), lax.axis_index("zh"), lax.axis_index("zl")
    tokens, grad = patches_in[0], grad_out[0]
    slot_rows = jnp.asarray(one_hot_rows(slot_order()))
    plane_rows = jnp.asarray(one_hot_rows(plane_order()))

    phi = dot("dc,kc->dk", slot_params, slot_rows, BF16)
    logits = dot("md,dc->mc", tokens, phi)
    disp_prob = jax.nn.softmax(logits, axis=0)
    comb_prob = jax.nn.softmax(logits, axis=1)
    dispatch, combine = disp_prob.astype(BF16), comb_prob.astype(BF16)
    slot_in = dot("mc,md->cd", dispatch, tokens, BF16)
    d_slot_out = dot("mc,md->cd", combine, grad, BF16)

    first = jnp.concatenate([w_in, swap_core(w_in)], axis=2)
    second = jnp.concatenate([w_out, swap_core(w_out)], axis=1)
    hidden = w_in.shape[2]

    sent = to_experts(jnp.stack([slot_in, d_slot_out]), plane_rows, half, place)

    def through(rows, d_rows):
        preact = dot("erd,edh->erh", rows, first)
        hidden_act = gelu(preact).astype(BF16)
        out_part = dot("erh,ehd->erd", hidden_act, second, BF16)
        d_hidden = (dot("erd,ehd->erh", d_rows, second) * gelu_slope(preact)).astype(BF16)
        in_part = dot("erh,edh->erd", d_hidden, first, BF16)
        return hidden_act, d_hidden, out_part, in_part

    made = []

    def early(rows, d_rows):
        made.append(through(rows, d_rows))
        return made[0]

    near, far = gather_z(*sent, place, early)
    made.append(through(*far))
    rows, d_rows = (jnp.concatenate(pair, axis=1) for pair in zip(near, far))
    hidden_act, d_hidden = (jnp.concatenate(pair, axis=1) for pair in list(zip(*made))[:2])
    in_part = made[1][3]

    done = {}

    def work(step, arrived):
        if step == 2:
            done["second"] = dot("erh,erd->ehd", ordered(hidden_act, in_part), d_rows, BF16)
            return [done["second"]]
        if step == 3:
            done["first"] = dot("erd,erh->edh", rows, ordered(d_hidden, done["second"]), BF16)
            return [done["first"]]
        if step <= STEPS:
            return []
        give_second, give_first = swap_core(done["second"][:, hidden:]), swap_core(done["first"][:, :, hidden:])
        done["second"] = (done["second"][:, :hidden].astype(F32) + give_second.astype(F32)).astype(BF16)
        done["first"] = (done["first"][:, :, :hidden].astype(F32) + give_first.astype(F32)).astype(BF16)
        return [done["first"], done["second"]]

    slot_out, d_slot_in = to_images(*scatter_z(made[0][2:], made[1][2:], send_beside(made[0][2:]), place, work), plane_rows, half)
    grad_first, grad_second = done["first"], done["second"]

    layer_out = dot("mc,cd->md", combine, slot_out, BF16)
    d_comb = dot("md,cd->mc", grad, slot_out)
    d_logit_comb = (comb_prob * (d_comb - jnp.sum(d_comb * comb_prob, axis=1, keepdims=True))).astype(BF16)
    grad_x = dot("mc,dc->md", d_logit_comb, phi)
    grad_phi = dot("md,mc->dc", tokens, dot("mk,kc->mc", d_logit_comb, slot_rows, BF16))

    d_disp = dot("md,cd->mc", tokens, d_slot_in)
    d_logit_disp = (disp_prob * (d_disp - jnp.sum(d_disp * disp_prob, axis=0, keepdims=True))).astype(BF16)
    grad_x = grad_x + dot("mc,cd->md", dispatch, d_slot_in) + dot("mc,dc->md", d_logit_disp, phi)
    grad_phi = grad_phi + dot("md,mc->dc", tokens, dot("mk,kc->mc", d_logit_disp, slot_rows, BF16))
    grad_phi = total_over_devices(grad_phi, core)
    return layer_out[None], grad_x.astype(BF16)[None], grad_phi, grad_first, grad_second


def solution(mesh):
    fine = Mesh(mesh.devices.reshape(ZL, 2, NY, ZH, NX), ("zl", "core", "y", "zh", "x"))
    images = P((*DP, *EXPERT), None, None)
    placed = (images, P(), P(EXPERT, None, DP), P(EXPERT, DP, None), images)
    return jax.shard_map(
        on_device,
        mesh=fine,
        in_specs=placed,
        out_specs=(images, images, P(), placed[2], placed[3]),
        check_vma=False,
    )
```
